32 devices in a mesh: row: 8 (over y, x, core), col: 4 (over z).
Axes of the slice: x: 2, y: 2, z: 4, core: 2. Of those that a mesh axis runs over, the one named last changes fastest.
Arguments:
- slab_rows: bfloat16 [8832, 2208], P('row'), may hold values from -6 to 6
- slab_pattern: int32 [128, 32], P('row'), may hold values 0 or 1
- owned_rows: bfloat16 [2208, 4416], P(('row', 'col')), may hold values from -0.1875 to 0.1875
- owned_pattern: int32 [32, 64], P(('row', 'col')), may hold values 0 or 1
- placement: int32 [64], replicated, may hold values from 0 to 63, each once
Outputs:
- product: bfloat16 [8832, 4416], P('row', 'col')
The draws below stay inside these ranges and needn't reach their ends.
Inputs may be any that keep to these rules, and one draw needn't show every extreme that they name: `placement`: each block column appears once.
All inputs are finite; a program needn't handle non-finite values. No bound on the sum of `slab_pattern` or of `owned_pattern` on one device may be relied on, other than what follows from the above.
Results may differ from the reference program's by a relative error of at most 0.001.
Values may be sent and summed in bfloat16 or wider, within the bound.
No kernel may reach another device: no remote copies, remote signals or barrier semaphores. Data moves between devices by JAX's collectives and lax.ppermute only.
A program may use at most 192 MiB of HBM per device.

```python
import jax
import jax.numpy as jnp

BS = 69
SLAB = 128
KB = 32
NB = 64


def with_ends(values, own_key, smallest, top_value):
    shape = values.shape
    spot = [jax.random.randint(jax.random.fold_in(own_key, axis), (), 0, shape[axis]) for axis in range(len(shape))]
    values = values.at[tuple(spot)].set(smallest)
    longest = shape.index(max(shape))
    spot[longest] = (spot[longest] + 1) % shape[longest]
    return values.at[tuple(spot)].set(top_value)


def block_scale(stream_key, dims, shards, low, top_value):
    factor_of = 1.0
    for axis_at, blocks in shards:
        draws = jax.random.uniform(jax.random.fold_in(jax.random.fold_in(stream_key, 6), axis_at), (blocks,), jnp.float32, low / len(shards), top_value / len(shards))
        factor_of = factor_of * jnp.repeat(jnp.exp(draws), dims[axis_at] // blocks).reshape((-1,) + (1,) * (len(dims) - 1 - axis_at))
    return factor_of


def centred(stream_key, shape, scale, most, cuts=(), held_as=jnp.bfloat16):
    loudness = block_scale(stream_key, shape, cuts, -0.22, 0.18) if cuts else 1.0
    entries = jax.random.normal(stream_key, shape, jnp.float32) * scale * loudness
    return jnp.minimum(jnp.maximum(entries, -most), most).astype(held_as)


def setup_inputs(seed: int = 0) -> dict:
    arg_keys = jax.random.split(jax.random.key(seed), 6)
    slab_rows = centred(arg_keys[0], (SLAB * BS, KB * BS), 1.0, 6.0, ((0, 8),))
    slab_pattern = with_ends((jax.random.randint(arg_keys[1], (SLAB, KB), 0, 2) < 1).astype(jnp.int32), jax.random.fold_in(arg_keys[1], 1), 0, 1)
    owned_rows = centred(arg_keys[2], (KB * BS, NB * BS), (KB * BS // 2) ** -0.5, 0.1875, ((0, 32),))
    owned_pattern = with_ends((jax.random.randint(arg_keys[3], (KB, NB), 0, 2) < 1).astype(jnp.int32), jax.random.fold_in(arg_keys[3], 1), 0, 1)
    placement = jax.random.permutation(arg_keys[4], NB).astype(jnp.int32)
    return dict(slab_rows=slab_rows, slab_pattern=slab_pattern, owned_rows=owned_rows, owned_pattern=owned_pattern, placement=placement)


def reference(slab_rows, slab_pattern, owned_rows, owned_pattern, placement):
    slab_mask = slab_pattern[:, None, :, None].astype(jnp.bfloat16)
    left_side = (slab_rows.reshape(SLAB, BS, KB, BS) * slab_mask).reshape(SLAB * BS, KB * BS)
    owned_mask = owned_pattern[:, None, :, None].astype(jnp.bfloat16)
    right_blocks = owned_rows.reshape(KB, BS, NB, BS) * owned_mask
    right_side = jnp.take(right_blocks, placement, axis=2).reshape(KB * BS, NB * BS)
    return jnp.dot(left_side, right_side, preferred_element_type=jnp.float32).astype(jnp.bfloat16)
```

```python
import functools

import jax
import jax.numpy as jnp
from jax import lax
from jax.experimental import pallas as pl
from jax.experimental.pallas import tpu as pltpu
from jax.sharding import PartitionSpec as P

BS = 69
LANES = 128
UNIT = 72
SLOT = 80
DEPTH = 256
VMEM_LIMIT = 28 * 2**20
X_SPLIT = False


def up(n, m):
    return (n + m - 1) // m * m


def moved(load, start, at, width):
    base = start // LANES
    off = start - base * LANES
    first = load(base)
    second = load(base + 1)
    lane_at = at % LANES
    turn = lax.rem(lane_at - off + LANES, LANES)
    first = pltpu.roll(first, turn, 1)
    second = pltpu.roll(second, turn, 1)
    lane = lax.broadcasted_iota(jnp.int32, first.shape, 1)
    pieces = []
    tile = at // LANES
    lo, hi = lane_at, min(lane_at + width, LANES)
    pieces.append((tile, jnp.where(lane < LANES - off + lane_at, first, second), lo, hi))
    if lane_at + width > LANES:
        pieces.append((tile + 1, jnp.where(lane < lane_at - off, first, second), 0, lane_at + width - LANES))
    return pieces


def right_kernel(n_col, placement, pattern, rows, *outs):
    width = outs[0].shape[1]
    here = placement.shape[0] // n_col
    me = lax.axis_index("col")
    shape = (UNIT, LANES)
    lane = lax.broadcasted_iota(jnp.int32, shape, 1)
    real = lax.broadcasted_iota(jnp.int32, shape, 0) < BS

    def load(tile):
        return rows[:, pl.ds(pl.multiple_of(tile * LANES, LANES), LANES)].astype(jnp.float32)

    for step in range(n_col):
        tiles = [jnp.zeros(shape, jnp.float32) for _ in range(width // LANES)]
        for t in range(here):
            source = placement[(me ^ step) * here + t]
            keep = real & (jnp.full(shape, pattern[0, source]) > 0)
            for tile, value, lo, hi in moved(load, source * BS, t * BS, BS):
                tiles[tile] = jnp.where((lane >= lo) & (lane < hi) & keep, value, tiles[tile])
        for at, value in enumerate(tiles):
            outs[step][:, at * LANES : (at + 1) * LANES] = value.astype(jnp.bfloat16)


def right_units(owned_rows, owned_pattern, placement, n_col):
    columns = owned_rows.shape[1]
    width = up(columns // n_col, LANES)
    return pl.pallas_call(
        functools.partial(right_kernel, n_col),
        grid=(1,),
        out_shape=[jax.ShapeDtypeStruct((UNIT, width), jnp.bfloat16)] * n_col,
        in_specs=[
            pl.BlockSpec(memory_space=pltpu.SMEM),
            pl.BlockSpec(memory_space=pltpu.SMEM),
            pl.BlockSpec((UNIT, up(columns, LANES) + LANES), lambda i: (0, 0)),
        ],
        out_specs=[pl.BlockSpec((UNIT, width), lambda i: (0, 0))] * n_col,
        compiler_params=pltpu.CompilerParams(vmem_limit_bytes=VMEM_LIMIT),
        name="right_units",
    )(placement, owned_pattern, owned_rows)


def place(slot):
    return slot // 3 * DEPTH + slot % 3 * SLOT


def left_kernel(n_col, columns, masks, pattern, rows, *refs):
    outs, pick, by_block = refs[:n_col], refs[-2], refs[-1]
    core = lax.axis_index("row") & 1
    block_rows, depth = pattern.shape
    high, width = outs[0].shape
    mine = [lax.axis_index("row") ^ jnp.where(core == 0, m0, m1) for m0, m1 in masks]
    blocks = [[m * n_col + (lax.axis_index("col") ^ step) for m in mine] for step in range(n_col)]

    @pl.when(pl.program_id(0) == 0)
    def _():
        lane = lax.broadcasted_iota(jnp.int32, (depth, width), 1)
        which = lax.broadcasted_iota(jnp.int32, (depth, width), 0)
        col = lax.broadcasted_iota(jnp.int32, (DEPTH, DEPTH), 1)
        ahead = lax.broadcasted_iota(jnp.int32, (DEPTH, DEPTH), 0) - col
        some = pattern[...].astype(jnp.bfloat16)
        for step in range(n_col):
            chosen = jnp.full((depth, width), -1, jnp.int32)
            for t, block in enumerate(blocks[step]):
                chosen = jnp.where((lane >= place(t)) & (lane < place(t) + BS), block, chosen)
                off = lax.rem(block * BS, LANES)
                at = t % 3 * SLOT
                hit = (ahead == off - at) & (col >= at) & (col < at + BS)
                pick[step * len(masks) + t] = jnp.where(hit, 1.0, 0.0).astype(jnp.bfloat16)
            spread = jnp.where(chosen == which, 1.0, 0.0).astype(jnp.bfloat16)
            by_block[step] = jnp.dot(some, spread, preferred_element_type=jnp.float32).astype(jnp.bfloat16)

    row = lax.broadcasted_iota(jnp.int32, (high, block_rows), 0) + pl.program_id(0) * high
    owner = lax.broadcasted_iota(jnp.int32, (high, block_rows), 1) * BS
    owned = jnp.where((row >= owner) & (row < owner + BS), 1.0, 0.0).astype(jnp.bfloat16)
    lane = lax.broadcasted_iota(jnp.int32, (high, DEPTH), 1)
    for step in range(n_col):
        for first in range(0, len(masks), 3):
            total = jnp.zeros((high, DEPTH), jnp.float32)
            for t in range(first, min(first + 3, len(masks))):
                tile = blocks[step][t] * BS // LANES
                part = rows[:, pl.ds(pl.multiple_of(tile * LANES, LANES), DEPTH)]
                part = jnp.where(lane < columns - tile * LANES, part, jnp.zeros_like(part))
                total += jnp.dot(part, pick[step * len(masks) + t], preferred_element_type=jnp.float32)
            at = first // 3 * DEPTH
            keep = jnp.dot(owned, by_block[step, :, at : at + DEPTH], preferred_element_type=jnp.float32)
            outs[step][:, at : at + DEPTH] = jnp.where(keep > 0.5, total, 0.0).astype(jnp.bfloat16)


def left_sides(slab_rows, slab_pattern, n_col, masks):
    height, columns = slab_rows.shape
    width = up(len(masks), 3) // 3 * DEPTH
    wide = up(columns, LANES) + LANES
    high = next(h for h in (368, 48, 16) if height % h == 0 and h * (wide + n_col * width) * 4 <= 12 * 2**20)
    return pl.pallas_call(
        functools.partial(left_kernel, n_col, columns, masks),
        grid=(height // high,),
        out_shape=[jax.ShapeDtypeStruct((height, width), jnp.bfloat16)] * n_col,
        in_specs=[
            pl.BlockSpec(slab_pattern.shape, lambda i: (0, 0)),
            pl.BlockSpec((high, wide), lambda i: (i, 0)),
        ],
        out_specs=[pl.BlockSpec((high, width), lambda i: (i, 0))] * n_col,
        scratch_shapes=[
            pltpu.VMEM((n_col * len(masks), DEPTH, DEPTH), jnp.bfloat16),
            pltpu.VMEM((n_col, slab_pattern.shape[0], width), jnp.bfloat16),
        ],
        compiler_params=pltpu.CompilerParams(vmem_limit_bytes=VMEM_LIMIT),
        cost_estimate=pl.CostEstimate(flops=height * n_col * len(masks) * DEPTH * DEPTH * 2, bytes_accessed=height * (columns + n_col * width) * 2, transcendentals=0),
        name="left_sides",
    )(slab_pattern, slab_rows)


def multiply_kernel(parts, with_total, *refs):
    lefts, places, n_pieces = parts
    pieces = refs[lefts : lefts + n_pieces]
    total = refs[lefts + n_pieces] if with_total else None
    out, right = refs[-2], refs[-1]

    @pl.when(pl.program_id(0) == 0)
    def _():
        right[...] = jnp.zeros_like(right)
        for at, piece, unit in places:
            right[at : at + UNIT, :] = pieces[piece][unit * UNIT : (unit + 1) * UNIT, :]

    width = refs[0].shape[1]
    value = total[...] if with_total else None
    for i in range(lefts):
        part = jnp.dot(refs[i][...], right[i * width : (i + 1) * width, :], preferred_element_type=jnp.float32)
        value = part if value is None else value + part
    out[...] = value[:, : out.shape[1]].astype(out.dtype)


def multiply(lefts, parts, total, columns, dtype):
    height, width = lefts[0].shape
    pieces, places = [], []
    base = 0
    for steps, group in parts:
        for slots, piece in group:
            for unit, (step, slot) in enumerate((step, slot) for slot in slots for step in range(steps)):
                places.append(((base + step) * width + place(slot), len(pieces), unit))
            pieces.append(piece)
        base += steps
    high = 368
    operands = [*lefts, *pieces]
    whole = lambda a: pl.BlockSpec(a.shape, lambda i: (0, 0))
    rows = lambda a: pl.BlockSpec((high, a.shape[1]), lambda i: (i, 0))
    in_specs = [rows(a) for a in lefts] + [whole(a) for a in pieces]
    if total is not None:
        operands.append(total)
        in_specs.append(rows(total))
    wide = pieces[0].shape[1]
    out = jax.ShapeDtypeStruct((height, columns if dtype == jnp.bfloat16 else wide), dtype)
    return pl.pallas_call(
        functools.partial(multiply_kernel, (len(lefts), places, len(pieces)), total is not None),
        grid=(height // high,),
        out_shape=out,
        in_specs=in_specs,
        out_specs=rows(out),
        scratch_shapes=[pltpu.VMEM((width * len(lefts), wide), jnp.bfloat16)],
        compiler_params=pltpu.CompilerParams(vmem_limit_bytes=VMEM_LIMIT),
        cost_estimate=pl.CostEstimate(flops=2 * height * width * len(lefts) * wide, bytes_accessed=height * columns * 4, transcendentals=0),
        name="multiply",
    )(*operands)


def per_device(n_row, n_col, slab_rows, slab_pattern, owned_rows, owned_pattern, placement):
    columns = owned_rows.shape[1] // n_col
    bits = [1 << b for b in range(1, n_row.bit_length() - 1)]
    orders = (bits, bits[::-1])

    def along_row(value, move):
        return lax.ppermute(value, "row", [(i, i ^ move[i & 1]) for i in range(n_row)])

    units = right_units(owned_rows, owned_pattern, placement, n_col)
    arrived = [units[0]]
    for step in range(1, n_col):
        arrived.append(lax.ppermute(units[step], "col", [(i, i ^ step) for i in range(n_col)]))

    masks = [(0, 0)]
    for move in zip(*orders):
        masks += [(m[0] ^ move[0], m[1] ^ move[1]) for m in masks]
    masks += [(1 ^ m[1], 1 ^ m[0]) for m in masks]
    lefts = left_sides(slab_rows, slab_pattern, n_col, masks)

    def gathered(steps):
        first = jnp.concatenate([arrived[s] for s in steps]) if len(steps) > 1 else arrived[steps[0]]
        pieces = [((0,), first)]
        for move in zip(*orders):
            at = len(pieces)
            pieces += [((slots[0] + at,), along_row(value, move)) for slots, value in pieces]
        half = len(masks) // 2
        if X_SPLIT:
            pieces += [((slots[0] + half,), along_row(value, (1, 1))) for slots, value in pieces]
        else:
            every = jnp.concatenate([value for _, value in pieces])
            pieces.append((tuple(range(half, 2 * half)), along_row(every, (1, 1))))
        return len(steps), pieces

    GROUPS = [[step] for step in range(n_col)]
    most = max(1, 24 // len(masks))
    CALLS = [GROUPS[at : min(at + most, n_col - 1)] for at in range(0, n_col - 1, most)] + [GROUPS[-1:]]
    total = None
    for at, call in enumerate(CALLS):
        mine = [lefts[step] for group in call for step in group]
        last = at == len(CALLS) - 1
        total = multiply(mine, [gathered(group) for group in call], total, columns, jnp.bfloat16 if last else jnp.float32)
    return total


def solution(mesh):
    return jax.shard_map(
        functools.partial(per_device, mesh.shape["row"], mesh.shape["col"]),
        mesh=mesh,
        in_specs=(
            P("row", None),
            P("row", None),
            P(("row", "col"), None),
            P(("row", "col"), None),
            P(),
        ),
        out_specs=P("row", "col"),
        check_vma=False,
    )
```

```python
import functools

import jax
import jax.numpy as jnp
from jax import lax
from jax.experimental import pallas as pl
from jax.experimental.pallas import tpu as pltpu
from jax.sharding import PartitionSpec as P

BS = 69
LANES = 128
UNIT = 72
PACK = 16
DEPTH = 256
SLOT = 80


def up(n, m):
    return (n + m - 1) // m * m


def moved(load, start, at, width):
    base = start // LANES
    off = start - base * LANES
    first = load(base)
    second = load(base + 1)
    lane_at = at % LANES
    turn = lax.rem(lane_at - off + LANES, LANES)
    first = pltpu.roll(first, turn, 1)
    second = pltpu.roll(second, turn, 1)
    lane = lax.broadcasted_iota(jnp.int32, first.shape, 1)
    pieces = []
    tile = at // LANES
    lo, hi = lane_at, min(lane_at + width, LANES)
    pieces.append((tile, jnp.where(lane < LANES - off + lane_at, first, second), lo, hi))
    if lane_at + width > LANES:
        pieces.append((tile + 1, jnp.where(lane < lane_at - off, first, second), 0, lane_at + width - LANES))
    return pieces


def limit(need):
    return pltpu.CompilerParams(vmem_limit_bytes=min(need + 8 * 2**20, 60 * 2**20))


def crossed(mask):
    return (1 ^ mask[1], 1 ^ mask[0])


def tie(values):
    arrays = [v[0] if isinstance(v, tuple) else v for v in values]
    arrays = lax.optimization_barrier(tuple(arrays))
    return tuple((a, v[1]) if isinstance(v, tuple) else a for a, v in zip(arrays, values))


def right_kernel(n_col, steps, scalars, raw, *refs):
    outs, rows = refs[-1 - len(steps) : -1], refs[-1]
    rows[: raw.shape[0], : raw.shape[1]] = raw[...]
    width = outs[0].shape[1]
    here = scalars.shape[1] // n_col
    me = lax.axis_index("col")
    shape = (UNIT, LANES)
    lane = lax.broadcasted_iota(jnp.int32, shape, 1)
    real = lax.broadcasted_iota(jnp.int32, shape, 0) < BS

    def load(tile):
        return rows[:, pl.ds(pl.multiple_of(tile * LANES, LANES), LANES)].astype(jnp.float32)

    for out, step in zip(outs, steps):
        tiles = [jnp.zeros(shape, jnp.float32) for _ in range(width // LANES)]
        for t in range(here):
            source = scalars[0, (me ^ step) * here + t]
            keep = real & (jnp.full(shape, scalars[1, source]) > 0)
            for tile, value, lo, hi in moved(load, source * BS, t * BS, BS):
                tiles[tile] = jnp.where((lane >= lo) & (lane < hi) & keep, value, tiles[tile])
        for at, value in enumerate(tiles):
            out[:, at * LANES : (at + 1) * LANES] = value.astype(jnp.bfloat16)


def right_units(scalars, owned_rows, n_col, steps, after=()):
    columns = owned_rows.shape[1]
    width = up(columns // n_col, LANES)
    return pl.pallas_call(
        functools.partial(right_kernel, n_col, steps),
        out_shape=[jax.ShapeDtypeStruct((UNIT, width), jnp.bfloat16)] * len(steps),
        in_specs=[pl.BlockSpec(memory_space=pltpu.SMEM)] + [pl.BlockSpec(memory_space=pltpu.VMEM)] * (1 + len(after)),
        out_specs=[pl.BlockSpec(memory_space=pltpu.VMEM)] * len(steps),
        scratch_shapes=[pltpu.VMEM((UNIT, up(columns, LANES) + LANES), jnp.bfloat16)],
        compiler_params=limit(2**22),
        cost_estimate=pl.CostEstimate(flops=8 * 10**9, bytes_accessed=0, transcendentals=0),
        name="right_units",
    )(scalars, owned_rows, *after)


def left_kernel(high, pattern, rows_in, out, rows, sems):
    height, columns = rows_in.shape
    block_rows, depth = pattern.shape
    width = out.shape[1]
    count = height // high

    def copy(i):
        return pltpu.make_async_copy(rows_in.at[pl.ds(i * high, high), :], rows.at[pl.ds(i * high, high), :], sems.at[i])

    for i in range(count):
        copy(i).start()
    lane = lax.broadcasted_iota(jnp.int32, (depth, width), 1)
    block = lax.broadcasted_iota(jnp.int32, (depth, width), 0) * BS
    spread = jnp.where((lane >= block) & (lane < block + BS), 1.0, 0.0).astype(jnp.bfloat16)
    by_block = jnp.dot(pattern[...].astype(jnp.bfloat16), spread, preferred_element_type=jnp.float32)
    for at in range(0, width, LANES):
        wide = min(LANES, columns - at)
        if wide <= 0:
            out[:, at:] = jnp.zeros((height, width - at), jnp.bfloat16)
            break
        if wide < LANES:
            out[:, at : at + LANES] = jnp.zeros((height, LANES), jnp.bfloat16)
    row = lax.broadcasted_iota(jnp.int32, (PACK, columns), 0)
    keeps = {}

    def keep(b):
        if b not in keeps:
            keeps.clear()
            keeps[b] = jnp.broadcast_to(by_block[b : b + 1, :columns], (PACK, columns)).astype(jnp.bfloat16)
        return keeps[b]

    for first in range(0, height, PACK):
        if first % high == 0:
            copy(first // high).wait()
        own, edge = first // BS, (first // BS + 1) * BS
        mask = keep(own)
        if edge < first + PACK:
            mask = jnp.where(row < edge - first, mask, keep(own + 1))
        out[first : first + PACK, :columns] = rows[first : first + PACK, :] * mask


def left_side(slab_rows, slab_pattern, width):
    height, columns = slab_rows.shape
    high = 368
    return pl.pallas_call(
        functools.partial(left_kernel, high),
        out_shape=jax.ShapeDtypeStruct((height, width), jnp.bfloat16),
        in_specs=[pl.BlockSpec(memory_space=pltpu.VMEM), pl.BlockSpec(memory_space=pltpu.HBM)],
        out_specs=pl.BlockSpec(memory_space=pltpu.VMEM),
        scratch_shapes=[pltpu.VMEM((height, columns), jnp.bfloat16), pltpu.SemaphoreType.DMA((height // high,))],
        compiler_params=limit(height * (width + columns) * 2),
        cost_estimate=pl.CostEstimate(flops=1, bytes_accessed=1, transcendentals=0),
        name="left_side",
    )(slab_pattern, slab_rows)


def place(slot):
    return slot // 3 * DEPTH + slot % 3 * SLOT


def side_kernel(n_col, groups, left, point, *refs):
    outs, pick = refs[: len(groups)], refs[-1]
    high = 368
    col = lax.broadcasted_iota(jnp.int32, (DEPTH, DEPTH), 1)
    ahead = lax.broadcasted_iota(jnp.int32, (DEPTH, DEPTH), 0) - col
    turn = 0
    for out, slots in zip(outs, groups):
        for first in range(0, len(slots), 3):
            tiles = []
            base = turn % 2 * 3 * DEPTH
            turn += 1
            for t, (mask, step) in enumerate(slots[first : first + 3]):
                start = block_of(n_col, mask, step) * BS
                tile = start // LANES
                tiles.append(pl.multiple_of(tile * LANES, LANES))
                at = t * SLOT
                hit = (ahead == start - tile * LANES - at) & (col >= at) & (col < at + BS)
                pick[base + t * DEPTH : base + (t + 1) * DEPTH, :] = jnp.where(hit, 1.0, 0.0).astype(jnp.bfloat16)
            for at in range(0, left.shape[0], high):
                total = None
                for t, tile in enumerate(tiles):
                    some = pick[base + t * DEPTH : base + (t + 1) * DEPTH, :]
                    part = jnp.dot(left[at : at + high, pl.ds(tile, DEPTH)], some, preferred_element_type=jnp.float32)
                    total = part if total is None else total + part
                out[at : at + high, first // 3 * DEPTH : (first // 3 + 1) * DEPTH] = total.astype(jnp.bfloat16)


def sides(left, n_col, groups, point):
    height = left.shape[0]
    widths = [up(len(slots), 3) // 3 * DEPTH for slots in groups]
    return pl.pallas_call(
        functools.partial(side_kernel, n_col, groups),
        out_shape=[jax.ShapeDtypeStruct((height, width), jnp.bfloat16) for width in widths],
        in_specs=[pl.BlockSpec(memory_space=pltpu.VMEM), pl.BlockSpec(memory_space=pl.ANY)],
        out_specs=[pl.BlockSpec(memory_space=pltpu.VMEM)] * len(groups),
        scratch_shapes=[pltpu.VMEM((6 * DEPTH, DEPTH), jnp.bfloat16)],
        compiler_params=limit(height * (sum(widths) + left.shape[1]) * 2),
        cost_estimate=pl.CostEstimate(flops=1, bytes_accessed=1, transcendentals=0),
        name="sides",
    )(left, point)


def block_of(n_col, mask, step):
    me = lax.axis_index("row")
    return (me ^ jnp.where(me & 1 == 0, mask[0], mask[1])) * n_col + (lax.axis_index("col") ^ step)


def listed(units):
    pieces, places = [], []
    for piece, *_ in units:
        at = next((i for i, p in enumerate(pieces) if p is piece), None)
        if at is None:
            at = len(pieces)
            pieces.append(piece)
        places.append(at)
    return pieces, places


def multiply_kernel(places, with_total, final, left, *refs):
    out, right = refs[len(refs) - 4 :][:2] if final else refs[-2:]
    pieces = refs[with_total:]
    right[...] = jnp.zeros_like(right)
    for slot, (piece, unit) in enumerate(places):
        right[place(slot) : place(slot) + UNIT, :] = pieces[piece][unit * UNIT : (unit + 1) * UNIT, :]
    high = 368
    copies = []
    for at in range(0, left.shape[0], high):
        value = jnp.dot(left[at : at + high, :], right[...], preferred_element_type=jnp.float32)
        if with_total:
            value += refs[0][at : at + high, :]
        if final:
            tiles, sems = refs[-2:]
            tiles[at : at + high, :] = value[:, : tiles.shape[1]].astype(tiles.dtype)
            copies.append(pltpu.make_async_copy(tiles.at[pl.ds(at, high)], out.at[pl.ds(at, high)], sems.at[at // high]))
            copies[-1].start()
        else:
            out[at : at + high, :] = value
    for copy in copies:
        copy.wait()


def multiply(left, total, units, columns=None, after=()):
    height, width = left.shape
    final = columns is not None
    pieces, places = listed(units)
    wide = pieces[0].shape[1]
    operands = [left] + ([] if total is None else [total]) + pieces
    memory = [pltpu.VMEM] * len(operands) + [pl.ANY] * len(after)
    scratch = [pltpu.VMEM((width, wide), jnp.bfloat16)]
    if final:
        scratch += [pltpu.VMEM((height, columns), jnp.bfloat16), pltpu.SemaphoreType.DMA((height // 368,))]
    return pl.pallas_call(
        functools.partial(multiply_kernel, [(at, unit[1]) for at, unit in zip(places, units)], total is not None, final),
        out_shape=jax.ShapeDtypeStruct((height, columns if final else wide), jnp.bfloat16 if final else jnp.float32),
        in_specs=[pl.BlockSpec(memory_space=space) for space in memory],
        out_specs=pl.BlockSpec(memory_space=pltpu.HBM if final else pltpu.VMEM),
        scratch_shapes=scratch,
        input_output_aliases={} if final or total is None else {1: 0},
        compiler_params=limit(width * wide * 2 + height * (wide * 6 + width * 2) + sum(p.size for p in pieces) * 2),
        cost_estimate=pl.CostEstimate(flops=1, bytes_accessed=1, transcendentals=0),
        name="multiply",
    )(*operands, *after)


def mark_kernel(value, out):
    pass


def mark(value, weight=3):
    return pl.pallas_call(
        mark_kernel,
        out_shape=jax.ShapeDtypeStruct(value.shape, value.dtype),
        in_specs=[pl.BlockSpec(memory_space=pl.ANY)],
        out_specs=pl.BlockSpec(memory_space=pl.ANY),
        input_output_aliases={0: 0},
        compiler_params=pltpu.CompilerParams(vmem_limit_bytes=2**20),
        cost_estimate=pl.CostEstimate(flops=weight * 10**9, bytes_accessed=1, transcendentals=0),
        name="mark",
    )(value)


def per_device(n_row, n_col, slab_rows, slab_pattern, owned_rows, owned_pattern, placement):
    columns = owned_rows.shape[1] // n_col
    bits = [1 << b for b in range(1, n_row.bit_length() - 1)]
    moves = list(zip(bits, bits[::-1]))
    last, deep = n_col - 1, len(moves)

    def along_row(value, move):
        return lax.ppermute(value, "row", [(i, i ^ move[i & 1]) for i in range(n_row)])

    def along_col(value, step):
        return lax.ppermute(value, "col", [(i, i ^ step) for i in range(n_col)])

    masks = [(0, 0)]
    for move in moves:
        masks += [(m[0] ^ move[0], m[1] ^ move[1]) for m in masks]

    full = len(masks) - 1

    def unit_of(key):
        value, unit = pieces[key]
        return value if value.shape[0] == UNIT else value[unit * UNIT : (unit + 1) * UNIT]

    def joined(keys):
        value = pieces[keys[0]][0]
        if value.shape[0] == UNIT * len(keys) and all(pieces[k][0] is value and pieces[k][1] == i for i, k in enumerate(keys)):
            return value
        return jnp.concatenate([unit_of(key) for key in keys]) if len(keys) > 1 else unit_of(keys[0])

    def hop(at, keys):
        sent = along_row(joined(keys), moves[at])
        for unit, (step, way) in enumerate(keys):
            pieces[step, way | 1 << at] = (sent, unit)

    def swap(keys):
        other = along_row(joined(keys), (1, 1))
        for unit, key in enumerate(keys):
            swaps[key] = (other, unit)

    def tied(keys, swapped, extra):
        sets = [(pieces, key) for key in keys] + [(swaps, key) for key in swapped]
        arrays = []
        for held, key in sets:
            if not any(held[key][0] is a for a in arrays):
                arrays.append(held[key][0])
        new = lax.optimization_barrier((*arrays, *extra))
        for old, fresh in zip(arrays, new):
            for held in (pieces, swaps):
                for key, (value, unit) in held.items():
                    if value is old:
                        held[key] = (fresh, unit)
        return new[len(arrays) :]

    ways = list(range(len(masks)))
    first, rest = [0, 1], list(range(2, n_col))
    scalars = jnp.concatenate([placement[None], owned_pattern])
    units = right_units(scalars, owned_rows, n_col, list(range(n_col)))

    pieces, swaps = {(0, 0): (units[0], 0)}, {}
    for step in range(1, n_col):
        pieces[step, 0] = (along_col(units[step], step), 0)

    def brought_by(step, way):
        return (step not in first) + way.bit_count() - 1

    def wave(number):
        for at in range(deep):
            keys = [(step, way) for step in rest + first for way in range(1 << at)]
            keys = [key for key in keys if brought_by(*key) == number - 1]
            if keys:
                hop(at, keys)

    def come(number):
        return [(step, way) for step in rest + first for way in ways[1:] if brought_by(step, way) == number]

    def own(keys):
        return [(*pieces[step, way], masks[way], step) for step, way in keys]

    def other(keys):
        return [(*swaps[step, way], crossed(masks[way]), step) for step, way in keys]

    def slots(keys, swapped):
        return [(masks[way], step) for step, way in keys] + [(crossed(masks[way]), step) for step, way in swapped]

    early = [(step, 0) for step in first] + come(0)
    arrived = [(step, 0) for step in rest]
    late = sum([come(number) for number in range(1, deep)], [])
    tail = come(deep)
    ready = early + arrived
    soon = [key for key in late if key[1] <= full // 2 and key[0] in rest]
    then = [key for key in late if key not in soon]
    groups = [(ready, []), (late, ready), ([], late), (tail, tail)]

    left = left_side(slab_rows, slab_pattern, up(slab_rows.shape[1], 2 * LANES))
    left, point = tied([(1, 0)], [], [left, scalars])
    point = mark(point)
    (point,) = tied([(0, 0), (1, 0)], [], [point])
    wave(0)
    (ready_left,) = sides(left, n_col, [slots(*groups[0])], point)
    ready_left, left, point = tied(arrived, [], [ready_left, left, point])
    point = mark(point)
    (point,) = tied(come(0), [], [point])
    for number in range(1, deep):
        wave(number)
    swap(ready)
    lefts = sides(left, n_col, [slots(*group) for group in groups[1:]], point)
    total = multiply(ready_left, None, own(ready))
    total, point, *lefts = tied(soon, [], [total, point, *lefts])
    wave(deep)
    total, point = tied(then, [], [total, point])
    point = mark(point, 10)
    (point,) = tied([], ready, [point])
    swap(late)
    total = multiply(lefts[0], total, own(late) + other(ready), after=[point])
    total, point = tied(tail, [], [total, point])
    swap(tail)
    point = mark(point)
    (point,) = tied([], late, [point])
    total = multiply(lefts[1], total, other(late), after=[point])
    return multiply(lefts[2], total, own(tail) + other(tail), columns)


def solution(mesh):
    return jax.shard_map(
        functools.partial(per_device, mesh.shape["row"], mesh.shape["col"]),
        mesh=mesh,
        in_specs=(
            P("row", None),
            P("row", None),
            P(("row", "col"), None),
            P(("row", "col"), None),
            P(),
        ),
        out_specs=P("row", "col"),
        check_vma=False,
    )
```

```python
import functools

import jax
import jax.numpy as jnp
from jax import lax
from jax.experimental import pallas as pl
from jax.experimental.pallas import tpu as pltpu
from jax.sharding import PartitionSpec as P

BS = 69
LANES = 128
BODY = 64
UNIT = 72
PACK = 16
DEPTH = 256
SLOT = 80


def up(n, m):
    return (n + m - 1) // m * m


def moved(load, start, at, width):
    base = start // LANES
    off = start - base * LANES
    first, second = load(base), load(base + 1)
    lane = lax.broadcasted_iota(jnp.int32, first.shape, 1)
    lane_at = at % LANES
    value = pltpu.roll(jnp.where(lane >= off, first, second), lax.rem(lane_at - off + LANES, LANES), 1)
    tile = at // LANES
    pieces = [(tile, value, lane_at, min(lane_at + width, LANES))]
    if lane_at + width > LANES:
        pieces.append((tile + 1, value, 0, lane_at + width - LANES))
    return pieces


def limit(need):
    return pltpu.CompilerParams(vmem_limit_bytes=min(need + 8 * 2**20, 60 * 2**20))


def crossed(mask):
    return (1 ^ mask[1], 1 ^ mask[0])


def unit_size(columns):
    full, over = columns // LANES, columns % LANES
    return full * BODY // PACK + pl.cdiv(full, 2) + pl.cdiv(pl.cdiv(3 * over, LANES) * (UNIT // 3), PACK)


def pack_unit(out, tiles, columns):
    full, over = columns // LANES, columns % LANES
    at = 0
    for tile in tiles[:full]:
        for row in range(0, BODY, PACK):
            out[at] = tile[row : row + PACK].astype(jnp.bfloat16)
            at += 1
    for t in range(0, full, 2):
        pair = [tiles[t][BODY:], tiles[t + 1][BODY:] if t + 1 < full else jnp.zeros_like(tiles[t][BODY:])]
        out[at] = jnp.concatenate(pair, 0).astype(jnp.bfloat16)
        at += 1
    if not over:
        return
    third = UNIT // 3
    lane = lax.broadcasted_iota(jnp.int32, (third, LANES), 1)
    packed = [jnp.zeros((third, LANES), jnp.float32) for _ in range(pl.cdiv(3 * over, LANES))]
    for g in range(3):
        value = tiles[full][g * third : (g + 1) * third]
        t, shift = g * over // LANES, g * over % LANES
        if shift:
            value = pltpu.roll(value, shift, 1)
        packed[t] = jnp.where((lane >= shift) & (lane < shift + over), value, packed[t])
        if shift + over > LANES:
            packed[t + 1] = jnp.where(lane < shift + over - LANES, value, packed[t + 1])
    rows = jnp.concatenate(packed, 0)
    if rows.shape[0] % PACK:
        rows = jnp.concatenate([rows, jnp.zeros((PACK - rows.shape[0] % PACK, LANES), jnp.float32)], 0)
    for row in range(0, rows.shape[0], PACK):
        out[at] = rows[row : row + PACK].astype(jnp.bfloat16)
        at += 1


def unpack_unit(right, first, piece, at, columns):
    full, over = columns // LANES, columns % LANES
    for t in range(full):
        for row in range(0, BODY, PACK):
            right[first + row : first + row + PACK, t * LANES : (t + 1) * LANES] = piece[at]
            at += 1
    zero = jnp.zeros((PACK // 2, LANES), jnp.float32)
    for t in range(0, full, 2):
        pair = piece[at].astype(jnp.float32)
        at += 1
        for k in range(min(2, full - t)):
            half = jnp.concatenate([pair[k * PACK // 2 : (k + 1) * PACK // 2], zero], 0).astype(jnp.bfloat16)
            right[first + BODY : first + BODY + PACK, (t + k) * LANES : (t + k + 1) * LANES] = half
    if not over:
        return
    third = UNIT // 3
    count = pl.cdiv(3 * over, LANES)
    rows = jnp.concatenate([piece[at + i].astype(jnp.float32) for i in range(pl.cdiv(count * third, PACK))], 0)
    packed = [rows[i * third : (i + 1) * third] for i in range(count)]
    lane = lax.broadcasted_iota(jnp.int32, (third, LANES), 1)
    values = []
    for g in range(3):
        t, shift = g * over // LANES, g * over % LANES
        value = packed[t]
        if shift:
            value = pltpu.roll(value, LANES - shift, 1)
        if shift + over > LANES:
            value = jnp.where(lane < LANES - shift, value, pltpu.roll(packed[t + 1], LANES - shift, 1))
        values.append(value)
    values.append(zero)
    right[first : first + SLOT, full * LANES : (full + 1) * LANES] = jnp.concatenate(values, 0).astype(jnp.bfloat16)


def right_kernel(n_col, steps, scalars, raw, *refs):
    outs, rows = refs[-1 - len(steps) : -1], refs[-1]
    rows[: raw.shape[0], : raw.shape[1]] = raw[...]
    columns = raw.shape[1] // n_col
    here = scalars.shape[1] // n_col
    me = lax.axis_index("col")
    shape = (UNIT, LANES)
    lane = lax.broadcasted_iota(jnp.int32, shape, 1)
    real = lax.broadcasted_iota(jnp.int32, shape, 0) < BS

    def load(tile):
        return rows[:, pl.ds(pl.multiple_of(tile * LANES, LANES), LANES)].astype(jnp.float32)

    for out, step in zip(outs, steps):
        tiles = [jnp.zeros(shape, jnp.float32) for _ in range(pl.cdiv(columns, LANES))]
        for t in range(here):
            source = scalars[0, (me ^ step) * here + t]
            keep = real & (jnp.full(shape, scalars[1, source]) > 0)
            for tile, value, lo, hi in moved(load, source * BS, t * BS, BS):
                tiles[tile] = jnp.where((lane >= lo) & (lane < hi) & keep, value, tiles[tile])
        pack_unit(out, tiles, columns)


def right_units(scalars, owned_rows, n_col, steps, weight):
    columns = owned_rows.shape[1]
    size = unit_size(columns // n_col)
    return pl.pallas_call(
        functools.partial(right_kernel, n_col, steps),
        out_shape=[jax.ShapeDtypeStruct((size, PACK, LANES), jnp.bfloat16)] * len(steps),
        in_specs=[pl.BlockSpec(memory_space=pltpu.SMEM)] + [pl.BlockSpec(memory_space=pltpu.VMEM)],
        out_specs=[pl.BlockSpec(memory_space=pltpu.VMEM)] * len(steps),
        scratch_shapes=[pltpu.VMEM((UNIT, up(columns, LANES) + LANES), jnp.bfloat16)],
        compiler_params=limit(2**22),
        cost_estimate=pl.CostEstimate(flops=weight, bytes_accessed=1, transcendentals=0),
        name="right_units",
    )(scalars, owned_rows)


def left_kernel(high, pattern, rows_in, out, rows, sems):
    height, columns = rows_in.shape
    block_rows, depth = pattern.shape
    width = out.shape[1]
    count = height // high

    def copy(i):
        return pltpu.make_async_copy(rows_in.at[pl.ds(i * high, high), :], rows.at[pl.ds(i * high, high), :], sems.at[i])

    for i in range(count):
        copy(i).start()
    lane = lax.broadcasted_iota(jnp.int32, (depth, width), 1)
    block = lax.broadcasted_iota(jnp.int32, (depth, width), 0) * BS
    spread = jnp.where((lane >= block) & (lane < block + BS), 1.0, 0.0).astype(jnp.bfloat16)
    by_block = jnp.dot(pattern[...].astype(jnp.bfloat16), spread, preferred_element_type=jnp.float32)
    for at in range(0, width, LANES):
        wide = min(LANES, columns - at)
        if wide <= 0:
            out[:, at:] = jnp.zeros((height, width - at), jnp.bfloat16)
            break
        if wide < LANES:
            out[:, at : at + LANES] = jnp.zeros((height, LANES), jnp.bfloat16)
    row = lax.broadcasted_iota(jnp.int32, (PACK, columns), 0)
    keeps = {}

    def keep(b):
        if b not in keeps:
            keeps.clear()
            keeps[b] = jnp.broadcast_to(by_block[b : b + 1, :columns], (PACK, columns)).astype(jnp.bfloat16)
        return keeps[b]

    for first in range(0, height, PACK):
        if first % high == 0:
            copy(first // high).wait()
        own, edge = first // BS, (first // BS + 1) * BS
        mask = keep(own)
        if edge < first + PACK:
            mask = jnp.where(row < edge - first, mask, keep(own + 1))
        out[first : first + PACK, :columns] = rows[first : first + PACK, :] * mask


def left_side(slab_rows, slab_pattern, width):
    height, columns = slab_rows.shape
    high = 368
    return pl.pallas_call(
        functools.partial(left_kernel, high),
        out_shape=jax.ShapeDtypeStruct((height, width), jnp.bfloat16),
        in_specs=[pl.BlockSpec(memory_space=pltpu.VMEM), pl.BlockSpec(memory_space=pltpu.HBM)],
        out_specs=pl.BlockSpec(memory_space=pltpu.VMEM),
        scratch_shapes=[pltpu.VMEM((height, columns), jnp.bfloat16), pltpu.SemaphoreType.DMA((height // high,))],
        compiler_params=limit(height * (width + columns) * 2),
        cost_estimate=pl.CostEstimate(flops=1, bytes_accessed=1, transcendentals=0),
        name="left_side",
    )(slab_pattern, slab_rows)


def place(slot):
    return slot // 3 * DEPTH + slot % 3 * SLOT


def side_kernel(n_col, groups, left, point, *refs):
    outs, pick = refs[: len(groups)], refs[-1]
    high = 368
    col = lax.broadcasted_iota(jnp.int32, (DEPTH, DEPTH), 1)
    ahead = lax.broadcasted_iota(jnp.int32, (DEPTH, DEPTH), 0) - col
    turn = 0
    for out, slots in zip(outs, groups):
        for first in range(0, len(slots), 3):
            tiles = []
            base = turn % 2 * 3 * DEPTH
            turn += 1
            for t, (mask, step) in enumerate(slots[first : first + 3]):
                start = block_of(n_col, mask, step) * BS
                tile = start // LANES
                tiles.append(pl.multiple_of(tile * LANES, LANES))
                at = t * SLOT
                hit = (ahead == start - tile * LANES - at) & (col >= at) & (col < at + BS)
                pick[base + t * DEPTH : base + (t + 1) * DEPTH, :] = jnp.where(hit, 1.0, 0.0).astype(jnp.bfloat16)
            for at in range(0, left.shape[0], high):
                total = None
                for t, tile in enumerate(tiles):
                    some = pick[base + t * DEPTH : base + (t + 1) * DEPTH, :]
                    part = jnp.dot(left[at : at + high, pl.ds(tile, DEPTH)], some, preferred_element_type=jnp.float32)
                    total = part if total is None else total + part
                out[at : at + high, first // 3 * DEPTH : (first // 3 + 1) * DEPTH] = total.astype(jnp.bfloat16)


def sides(left, n_col, groups, point):
    height = left.shape[0]
    widths = [up(len(slots), 3) // 3 * DEPTH for slots in groups]
    return pl.pallas_call(
        functools.partial(side_kernel, n_col, groups),
        out_shape=[jax.ShapeDtypeStruct((height, width), jnp.bfloat16) for width in widths],
        in_specs=[pl.BlockSpec(memory_space=pltpu.VMEM), pl.BlockSpec(memory_space=pl.ANY)],
        out_specs=[pl.BlockSpec(memory_space=pltpu.VMEM)] * len(groups),
        scratch_shapes=[pltpu.VMEM((6 * DEPTH, DEPTH), jnp.bfloat16)],
        compiler_params=limit(height * (sum(widths) + left.shape[1]) * 2),
        cost_estimate=pl.CostEstimate(flops=1, bytes_accessed=1, transcendentals=0),
        name="sides",
    )(left, point)


def block_of(n_col, mask, step):
    me = lax.axis_index("row")
    return (me ^ jnp.where(me & 1 == 0, mask[0], mask[1])) * n_col + (lax.axis_index("col") ^ step)


def listed(units):
    pieces, places = [], []
    for piece, *_ in units:
        at = next((i for i, p in enumerate(pieces) if p is piece), None)
        if at is None:
            at = len(pieces)
            pieces.append(piece)
        places.append(at)
    return pieces, places


def row_tiles(height, final):
    starts = list(range(0, height, 368))
    if final and height - starts[-1] == 368:
        starts.append(height - 128)
    return [(at, end - at) for at, end in zip(starts, starts[1:] + [height])]


def multiply_kernel(places, columns, with_total, final, left, *refs):
    out, right = refs[len(refs) - 4 :][:2] if final else refs[-2:]
    pieces = refs[with_total:]
    right[...] = jnp.zeros_like(right)
    for slot, (piece, unit) in enumerate(places):
        unpack_unit(right, place(slot), pieces[piece], unit * unit_size(columns), columns)
    copies = []
    for at, high in row_tiles(left.shape[0], final):
        value = jnp.dot(left[at : at + high, :], right[...], preferred_element_type=jnp.float32)
        if with_total:
            value += refs[0][at : at + high, :]
        if final:
            tiles, sems = refs[-2:]
            tiles[at : at + high, :] = value[:, : tiles.shape[1]].astype(tiles.dtype)
            copies.append(pltpu.make_async_copy(tiles.at[pl.ds(at, high)], out.at[pl.ds(at, high)], sems.at[len(copies)]))
            copies[-1].start()
        else:
            out[at : at + high, :] = value
    for copy in copies:
        copy.wait()


def multiply(left, total, units, columns, final=False, after=()):
    height, width = left.shape
    pieces, places = listed(units)
    wide = up(columns, LANES)
    operands = [left] + ([] if total is None else [total]) + pieces
    memory = [pltpu.VMEM] * len(operands) + [pl.ANY] * len(after)
    scratch = [pltpu.VMEM((width, wide), jnp.bfloat16)]
    if final:
        scratch += [pltpu.VMEM((height, columns), jnp.bfloat16), pltpu.SemaphoreType.DMA((len(row_tiles(height, True)),))]
    return pl.pallas_call(
        functools.partial(multiply_kernel, [(at, unit[1]) for at, unit in zip(places, units)], columns, total is not None, final),
        out_shape=jax.ShapeDtypeStruct((height, columns if final else wide), jnp.bfloat16 if final else jnp.float32),
        in_specs=[pl.BlockSpec(memory_space=space) for space in memory],
        out_specs=pl.BlockSpec(memory_space=pltpu.HBM if final else pltpu.VMEM),
        scratch_shapes=scratch,
        compiler_params=limit(width * wide * 2 + height * (wide * 6 + width * 2) + sum(p.size for p in pieces) * 2),
        cost_estimate=pl.CostEstimate(flops=1, bytes_accessed=1, transcendentals=0),
        name="multiply",
    )(*operands, *after)


def mark_kernel(value, out):
    pass


def mark(value, weight=3):
    return pl.pallas_call(
        mark_kernel,
        out_shape=jax.ShapeDtypeStruct(value.shape, value.dtype),
        in_specs=[pl.BlockSpec(memory_space=pl.ANY)],
        out_specs=pl.BlockSpec(memory_space=pl.ANY),
        input_output_aliases={0: 0},
        compiler_params=pltpu.CompilerParams(vmem_limit_bytes=2**20),
        cost_estimate=pl.CostEstimate(flops=weight * 10**9, bytes_accessed=1, transcendentals=0),
        name="mark",
    )(value)


def per_device(n_row, n_col, slab_rows, slab_pattern, owned_rows, owned_pattern, placement):
    columns = owned_rows.shape[1] // n_col
    size = unit_size(columns)
    bits = [1 << b for b in range(1, n_row.bit_length() - 1)]
    moves = list(zip(bits, bits[::-1]))
    last, deep = n_col - 1, len(moves)

    def along_row(value, move):
        return lax.ppermute(value, "row", [(i, i ^ move[i & 1]) for i in range(n_row)])

    def along_col(value, step):
        return lax.ppermute(value, "col", [(i, i ^ step) for i in range(n_col)])

    masks = [(0, 0)]
    for move in moves:
        masks += [(m[0] ^ move[0], m[1] ^ move[1]) for m in masks]

    full = len(masks) - 1

    def unit_of(key):
        value, unit = pieces[key]
        return value if value.shape[0] == size else value[unit * size : (unit + 1) * size]

    def joined(keys):
        value = pieces[keys[0]][0]
        if value.shape[0] == size * len(keys) and all(pieces[k][0] is value and pieces[k][1] == i for i, k in enumerate(keys)):
            return value
        return jnp.concatenate([unit_of(key) for key in keys]) if len(keys) > 1 else unit_of(keys[0])

    def hop(at, keys):
        sent = along_row(joined(keys), moves[at])
        for unit, (step, way) in enumerate(keys):
            pieces[step, way | 1 << at] = (sent, unit)

    def swap(keys):
        other = along_row(joined(keys), (1, 1))
        for unit, key in enumerate(keys):
            swaps[key] = (other, unit)

    def tied(keys, swapped, extra):
        sets = [(pieces, key) for key in keys] + [(swaps, key) for key in swapped]
        arrays = []
        for held, key in sets:
            if not any(held[key][0] is a for a in arrays):
                arrays.append(held[key][0])
        new = lax.optimization_barrier((*arrays, *extra))
        for old, fresh in zip(arrays, new):
            for held in (pieces, swaps):
                for key, (value, unit) in held.items():
                    if value is old:
                        held[key] = (fresh, unit)
        return new[len(arrays) :]

    ways = list(range(len(masks)))
    first, rest = [0, 1], list(range(2, n_col))
    scalars = jnp.concatenate([placement[None], owned_pattern])
    units = right_units(scalars, owned_rows, n_col, list(range(1, n_col)), 8 * 10**9)
    units = right_units(scalars, owned_rows, n_col, [0], 1) + units

    pieces, swaps = {(0, 0): (units[0], 0)}, {}
    for step in range(1, n_col):
        pieces[step, 0] = (along_col(units[step], step), 0)

    def brought_by(step, way):
        return (step not in first) + way.bit_count() - 1

    def wave(number):
        for at in range(deep):
            keys = [(step, way) for step in rest + first for way in range(1 << at)]
            keys = [key for key in keys if brought_by(*key) == number - 1]
            if keys:
                hop(at, keys)

    def come(number):
        return [(step, way) for step in rest + first for way in ways[1:] if brought_by(step, way) == number]

    def own(keys):
        return [(*pieces[step, way], masks[way], step) for step, way in keys]

    def other(keys):
        return [(*swaps[step, way], crossed(masks[way]), step) for step, way in keys]

    def slots(keys, swapped):
        return [(masks[way], step) for step, way in keys] + [(crossed(masks[way]), step) for step, way in swapped]

    early = [(step, 0) for step in first] + come(0)
    arrived = [(step, 0) for step in rest]
    late = sum([come(number) for number in range(1, deep)], [])
    tail = come(deep)
    ready = early + arrived
    soon = [key for key in late if key[1] <= full // 2 and key[0] in rest]
    then = [key for key in late if key not in soon]
    groups = [(ready, []), ([], ready), (late, []), ([], late), (tail, tail)]

    left = left_side(slab_rows, slab_pattern, up(slab_rows.shape[1], 2 * LANES))
    left, point = tied([(1, 0)], [], [left, scalars])
    point = mark(point)
    (point,) = tied([(0, 0), (1, 0)], [], [point])
    wave(0)
    lefts = sides(left, n_col, [slots(*group) for group in groups], point)
    *lefts, point = tied(arrived, [], [*lefts, point])
    point = mark(point)
    (point,) = tied(come(0), [], [point])
    for number in range(1, deep):
        wave(number)
    swap(ready)
    total = multiply(lefts[0], None, own(ready), columns)
    total, point = tied(soon, [], [total, point])
    wave(deep)
    point = mark(point, 10)
    point, total = tied([], ready, [point, total])
    total = multiply(lefts[1], total, other(ready), columns, after=[point])
    (total,) = tied(then, [], [total])
    swap(late)
    total = multiply(lefts[2], total, own(late), columns)
    total, point = tied(tail, [], [total, point])
    swap(tail)
    point = mark(point, 10)
    (point,) = tied([], late, [point])
    total = multiply(lefts[3], total, other(late), columns, after=[point])
    return multiply(lefts[4], total, own(tail) + other(tail), columns, final=True)


def solution(mesh):
    return jax.shard_map(
        functools.partial(per_device, mesh.shape["row"], mesh.shape["col"]),
        mesh=mesh,
        in_specs=(
            P("row", None),
            P("row", None),
            P(("row", "col"), None),
            P(("row", "col"), None),
            P(),
        ),
        out_specs=P("row", "col"),
        check_vma=False,
    )
```

```python
import functools

import jax
import jax.numpy as jnp
from jax import lax
from jax.experimental import pallas as pl
from jax.experimental.pallas import tpu as pltpu
from jax.sharding import PartitionSpec as P

BS = 69
LANES = 128
BODY = 64
UNIT = 72
PACK = 16
DEPTH = 256
CODE = 1 << 16
SLOT = 80


def up(n, m):
    return (n + m - 1) // m * m


def moved(load, start, at, width):
    base = start // LANES
    off = start - base * LANES
    first, second = load(base), load(base + 1)
    lane = lax.broadcasted_iota(jnp.int32, first.shape, 1)
    lane_at = at % LANES
    value = pltpu.roll(jnp.where(lane >= off, first, second), lax.rem(lane_at - off + LANES, LANES), 1)
    tile = at // LANES
    pieces = [(tile, value, lane_at, min(lane_at + width, LANES))]
    if lane_at + width > LANES:
        pieces.append((tile + 1, value, 0, lane_at + width - LANES))
    return pieces


def limit(need):
    return pltpu.CompilerParams(vmem_limit_bytes=min(need + 8 * 2**20, 60 * 2**20))


def crossed(mask):
    return (1 ^ mask[1], 1 ^ mask[0])


def unit_size(columns):
    full, over = columns // LANES, columns % LANES
    return full * BODY // PACK + pl.cdiv(full, PACK // (BS - BODY)) + pl.cdiv(pl.cdiv(3 * over, LANES) * (UNIT // 3), PACK)


def pack_unit(out, tiles, columns):
    full, over = columns // LANES, columns % LANES
    at = 0
    for tile in tiles[:full]:
        for row in range(0, BODY, PACK):
            out[at] = tile[row : row + PACK].astype(jnp.bfloat16)
            at += 1
    few = BS - BODY
    for t in range(0, full, PACK // few):
        rows = jnp.zeros((PACK, LANES), jnp.float32)
        for k, tile in enumerate(tiles[t : min(full, t + PACK // few)]):
            rows += pltpu.roll(jnp.concatenate([tile[BODY:], jnp.zeros((PACK + BODY - UNIT, LANES), jnp.float32)], 0), k * few, 0)
        out[at] = rows.astype(jnp.bfloat16)
        at += 1
    if not over:
        return
    third = UNIT // 3
    lane = lax.broadcasted_iota(jnp.int32, (third, LANES), 1)
    packed = [jnp.zeros((third, LANES), jnp.float32) for _ in range(pl.cdiv(3 * over, LANES))]
    for g in range(3):
        value = tiles[full][g * third : (g + 1) * third]
        t, shift = g * over // LANES, g * over % LANES
        if shift:
            value = pltpu.roll(value, shift, 1)
        packed[t] = jnp.where((lane >= shift) & (lane < shift + over), value, packed[t])
        if shift + over > LANES:
            packed[t + 1] = jnp.where(lane < shift + over - LANES, value, packed[t + 1])
    rows = jnp.concatenate(packed, 0)
    if rows.shape[0] % PACK:
        rows = jnp.concatenate([rows, jnp.zeros((PACK - rows.shape[0] % PACK, LANES), jnp.float32)], 0)
    for row in range(0, rows.shape[0], PACK):
        out[at] = rows[row : row + PACK].astype(jnp.bfloat16)
        at += 1


def unpack_unit(right, first, piece, at, columns):
    full, over = columns // LANES, columns % LANES
    for t in range(full):
        for row in range(0, BODY, PACK):
            right[first + row : first + row + PACK, t * LANES : (t + 1) * LANES] = piece[at]
            at += 1
    few = BS - BODY
    row = lax.broadcasted_iota(jnp.int32, (PACK, LANES), 0)
    for t in range(0, full, PACK // few):
        rows = piece[at].astype(jnp.float32)
        at += 1
        for k in range(min(PACK // few, full - t)):
            mine = pltpu.roll(rows, PACK - k * few, 0) if k else rows
            mine = jnp.where(row < few, mine, 0.0).astype(jnp.bfloat16)
            right[first + BODY : first + BODY + PACK, (t + k) * LANES : (t + k + 1) * LANES] = mine
    if not over:
        return
    third = UNIT // 3
    count = pl.cdiv(3 * over, LANES)
    rows = jnp.concatenate([piece[at + i].astype(jnp.float32) for i in range(pl.cdiv(count * third, PACK))], 0)
    packed = [rows[i * third : (i + 1) * third] for i in range(count)]
    lane = lax.broadcasted_iota(jnp.int32, (third, LANES), 1)
    values = []
    for g in range(3):
        t, shift = g * over // LANES, g * over % LANES
        value = packed[t]
        if shift:
            value = pltpu.roll(value, LANES - shift, 1)
        if shift + over > LANES:
            value = jnp.where(lane < LANES - shift, value, pltpu.roll(packed[t + 1], LANES - shift, 1))
        values.append(value)
    values.append(jnp.zeros((SLOT - UNIT, LANES), jnp.float32))
    right[first : first + SLOT, full * LANES : (full + 1) * LANES] = jnp.concatenate(values, 0).astype(jnp.bfloat16)


def right_kernel(n_col, steps, scalars, raw, *refs):
    outs, rows = refs[-1 - len(steps) : -1], refs[-1]
    rows[: raw.shape[0], : raw.shape[1]] = raw[...]
    columns = raw.shape[1] // n_col
    here = scalars.shape[0] // n_col
    me = lax.axis_index("col")
    shape = (UNIT, LANES)
    lane = lax.broadcasted_iota(jnp.int32, shape, 1)
    real = lax.broadcasted_iota(jnp.int32, shape, 0) < BS

    def load(tile):
        return rows[:, pl.ds(pl.multiple_of(tile * LANES, LANES), LANES)].astype(jnp.float32)

    for out, step in zip(outs, steps):
        tiles = [jnp.zeros(shape, jnp.float32) for _ in range(pl.cdiv(columns, LANES))]
        for t in range(here):
            source = scalars[(me ^ step) * here + t] & (CODE - 1)
            keep = real & (jnp.full(shape, scalars[source]) >= CODE)
            for tile, value, lo, hi in moved(load, source * BS, t * BS, BS):
                tiles[tile] = jnp.where((lane >= lo) & (lane < hi) & keep, value, tiles[tile])
        pack_unit(out, tiles, columns)


def right_units(scalars, owned_rows, n_col, steps, weight):
    columns = owned_rows.shape[1]
    size = unit_size(columns // n_col)
    return pl.pallas_call(
        functools.partial(right_kernel, n_col, steps),
        out_shape=[jax.ShapeDtypeStruct((size, PACK, LANES), jnp.bfloat16)] * len(steps),
        in_specs=[pl.BlockSpec(memory_space=pltpu.SMEM)] + [pl.BlockSpec(memory_space=pltpu.VMEM)],
        out_specs=[pl.BlockSpec(memory_space=pltpu.VMEM)] * len(steps),
        scratch_shapes=[pltpu.VMEM((UNIT, up(columns, LANES) + LANES), jnp.bfloat16)],
        compiler_params=limit(2**22),
        cost_estimate=pl.CostEstimate(flops=weight, bytes_accessed=1, transcendentals=0),
        name="right_units",
    )(scalars, owned_rows)


def left_kernel(high, pattern, rows_in, out, rows, sems):
    height, columns = rows_in.shape
    block_rows, depth = pattern.shape
    width = out.shape[1]
    count = height // high

    def copy(i):
        return pltpu.make_async_copy(rows_in.at[pl.ds(i * high, high), :], rows.at[pl.ds(i * high, high), :], sems.at[i])

    for i in range(count):
        copy(i).start()
    lane = lax.broadcasted_iota(jnp.int32, (depth, width), 1)
    block = lax.broadcasted_iota(jnp.int32, (depth, width), 0) * BS
    spread = jnp.where((lane >= block) & (lane < block + BS), 1.0, 0.0).astype(jnp.bfloat16)
    by_block = jnp.dot(pattern[...].astype(jnp.bfloat16), spread, preferred_element_type=jnp.float32)
    for at in range(0, width, LANES):
        wide = min(LANES, columns - at)
        if wide <= 0:
            out[:, at:] = jnp.zeros((height, width - at), jnp.bfloat16)
            break
        if wide < LANES:
            out[:, at : at + LANES] = jnp.zeros((height, LANES), jnp.bfloat16)
    row = lax.broadcasted_iota(jnp.int32, (PACK, columns), 0)
    keeps = {}

    def keep(b):
        if b not in keeps:
            keeps.clear()
            keeps[b] = jnp.broadcast_to(by_block[b : b + 1, :columns], (PACK, columns)).astype(jnp.bfloat16)
        return keeps[b]

    for first in range(0, height, PACK):
        if first % high == 0:
            copy(first // high).wait()
        own, edge = first // BS, (first // BS + 1) * BS
        mask = keep(own)
        if edge < first + PACK:
            mask = jnp.where(row < edge - first, mask, keep(own + 1))
        out[first : first + PACK, :columns] = rows[first : first + PACK, :] * mask


def left_side(slab_rows, slab_pattern, width):
    height, columns = slab_rows.shape
    high = 368
    return pl.pallas_call(
        functools.partial(left_kernel, high),
        out_shape=jax.ShapeDtypeStruct((height, width), jnp.bfloat16),
        in_specs=[pl.BlockSpec(memory_space=pltpu.VMEM), pl.BlockSpec(memory_space=pltpu.HBM)],
        out_specs=pl.BlockSpec(memory_space=pltpu.VMEM),
        scratch_shapes=[pltpu.VMEM((height, columns), jnp.bfloat16), pltpu.SemaphoreType.DMA((height // high,))],
        compiler_params=limit(height * (width + columns) * 2),
        cost_estimate=pl.CostEstimate(flops=1, bytes_accessed=1, transcendentals=0),
        name="left_side",
    )(slab_pattern, slab_rows)


def place(slot):
    return slot // 3 * DEPTH + slot % 3 * SLOT


def side_kernel(n_col, groups, left, point, *refs):
    outs, pick = refs[: len(groups)], refs[-1]
    high = 368
    col = lax.broadcasted_iota(jnp.int32, (DEPTH, DEPTH), 1)
    ahead = lax.broadcasted_iota(jnp.int32, (DEPTH, DEPTH), 0) - col
    turn = 0
    for out, slots in zip(outs, groups):
        for first in range(0, len(slots), 3):
            tiles = []
            base = turn % 2 * 3 * DEPTH
            turn += 1
            for t, (mask, step) in enumerate(slots[first : first + 3]):
                start = block_of(n_col, mask, step) * BS
                tile = start // LANES
                tiles.append(pl.multiple_of(tile * LANES, LANES))
                at = t * SLOT
                hit = (ahead == start - tile * LANES - at) & (col >= at) & (col < at + BS)
                pick[base + t * DEPTH : base + (t + 1) * DEPTH, :] = jnp.where(hit, 1.0, 0.0).astype(jnp.bfloat16)
            for at in range(0, left.shape[0], high):
                total = None
                for t, tile in enumerate(tiles):
                    some = pick[base + t * DEPTH : base + (t + 1) * DEPTH, :]
                    part = jnp.dot(left[at : at + high, pl.ds(tile, DEPTH)], some, preferred_element_type=jnp.float32)
                    total = part if total is None else total + part
                out[at : at + high, first // 3 * DEPTH : (first // 3 + 1) * DEPTH] = total.astype(jnp.bfloat16)


def sides(left, n_col, groups, point):
    height = left.shape[0]
    widths = [up(len(slots), 3) // 3 * DEPTH for slots in groups]
    return pl.pallas_call(
        functools.partial(side_kernel, n_col, groups),
        out_shape=[jax.ShapeDtypeStruct((height, width), jnp.bfloat16) for width in widths],
        in_specs=[pl.BlockSpec(memory_space=pltpu.VMEM), pl.BlockSpec(memory_space=pl.ANY)],
        out_specs=[pl.BlockSpec(memory_space=pltpu.VMEM)] * len(groups),
        scratch_shapes=[pltpu.VMEM((6 * DEPTH, DEPTH), jnp.bfloat16)],
        compiler_params=limit(height * (sum(widths) + left.shape[1]) * 2),
        cost_estimate=pl.CostEstimate(flops=1, bytes_accessed=1, transcendentals=0),
        name="sides",
    )(left, point)


def block_of(n_col, mask, step):
    me = lax.axis_index("row")
    return (me ^ jnp.where(me & 1 == 0, mask[0], mask[1])) * n_col + (lax.axis_index("col") ^ step)


def listed(units):
    pieces, places = [], []
    for piece, *_ in units:
        at = next((i for i, p in enumerate(pieces) if p is piece), None)
        if at is None:
            at = len(pieces)
            pieces.append(piece)
        places.append(at)
    return pieces, places


def row_tiles(height, final):
    starts = list(range(0, height, 368))
    if final and height - starts[-1] == 368:
        starts.append(height - 128)
    return [(at, end - at) for at, end in zip(starts, starts[1:] + [height])]


def multiply_kernel(places, columns, with_total, final, left, *refs):
    out, right = refs[len(refs) - 4 :][:2] if final else refs[-2:]
    pieces = refs[with_total:]
    for first in range(0, right.shape[0], DEPTH):
        used = min(3, len(places) - first // DEPTH * 3) * SLOT
        right[first + used : first + DEPTH, :] = jnp.zeros((DEPTH - used, right.shape[1]), right.dtype)
    for slot, (piece, unit) in enumerate(places):
        unpack_unit(right, place(slot), pieces[piece], unit * unit_size(columns), columns)
    copies = []
    for at, high in row_tiles(left.shape[0], final):
        value = jnp.dot(left[at : at + high, :], right[...], preferred_element_type=jnp.float32)
        if with_total:
            value += refs[0][at : at + high, :]
        if final:
            tiles, sems = refs[-2:]
            tiles[at : at + high, :] = value[:, : tiles.shape[1]].astype(tiles.dtype)
            copies.append(pltpu.make_async_copy(tiles.at[pl.ds(at, high)], out.at[pl.ds(at, high)], sems.at[len(copies)]))
            copies[-1].start()
        else:
            out[at : at + high, :] = value
    for copy in copies:
        copy.wait()


def multiply(left, total, units, columns, final=False, after=()):
    height, width = left.shape
    pieces, places = listed(units)
    wide = up(columns, LANES)
    operands = [left] + ([] if total is None else [total]) + pieces
    memory = [pltpu.VMEM] * len(operands) + [pl.ANY] * len(after)
    scratch = [pltpu.VMEM((width, wide), jnp.bfloat16)]
    if final:
        scratch += [pltpu.VMEM((height, columns), jnp.bfloat16), pltpu.SemaphoreType.DMA((len(row_tiles(height, True)),))]
    return pl.pallas_call(
        functools.partial(multiply_kernel, [(at, unit[1]) for at, unit in zip(places, units)], columns, total is not None, final),
        out_shape=jax.ShapeDtypeStruct((height, columns if final else wide), jnp.bfloat16 if final else jnp.float32),
        in_specs=[pl.BlockSpec(memory_space=space) for space in memory],
        out_specs=pl.BlockSpec(memory_space=pltpu.HBM if final else pltpu.VMEM),
        scratch_shapes=scratch,
        compiler_params=limit(width * wide * 2 + height * (wide * 6 + width * 2) + sum(p.size for p in pieces) * 2),
        cost_estimate=pl.CostEstimate(flops=1, bytes_accessed=1, transcendentals=0),
        name="multiply",
    )(*operands, *after)


def mark_kernel(value, out):
    pass


def mark(value, weight=3):
    return pl.pallas_call(
        mark_kernel,
        out_shape=jax.ShapeDtypeStruct(value.shape, value.dtype),
        in_specs=[pl.BlockSpec(memory_space=pl.ANY)],
        out_specs=pl.BlockSpec(memory_space=pl.ANY),
        input_output_aliases={0: 0},
        compiler_params=pltpu.CompilerParams(vmem_limit_bytes=2**20),
        cost_estimate=pl.CostEstimate(flops=weight * 10**9, bytes_accessed=1, transcendentals=0),
        name="mark",
    )(value)


def per_device(n_row, n_col, slab_rows, slab_pattern, owned_rows, owned_pattern, placement):
    columns = owned_rows.shape[1] // n_col
    size = unit_size(columns)
    bits = [1 << b for b in range(1, n_row.bit_length() - 1)]
    moves = list(zip(bits, bits[::-1]))
    last, deep = n_col - 1, len(moves)

    def along_row(value, move):
        return lax.ppermute(value, "row", [(i, i ^ move[i & 1]) for i in range(n_row)])

    def along_col(value, step):
        return lax.ppermute(value, "col", [(i, i ^ step) for i in range(n_col)])

    masks = [(0, 0)]
    for move in moves:
        masks += [(m[0] ^ move[0], m[1] ^ move[1]) for m in masks]

    full = len(masks) - 1

    def unit_of(key):
        value, unit = pieces[key]
        return value if value.shape[0] == size else value[unit * size : (unit + 1) * size]

    def joined(keys):
        value = pieces[keys[0]][0]
        if value.shape[0] == size * len(keys) and all(pieces[k][0] is value and pieces[k][1] == i for i, k in enumerate(keys)):
            return value
        return jnp.concatenate([unit_of(key) for key in keys]) if len(keys) > 1 else unit_of(keys[0])

    def hop(at, keys):
        sent = along_row(joined(keys), moves[at])
        for unit, (step, way) in enumerate(keys):
            pieces[step, way | 1 << at] = (sent, unit)

    def swap(keys):
        other = along_row(joined(keys), (1, 1))
        for unit, key in enumerate(keys):
            swaps[key] = (other, unit)

    def tied(keys, swapped, extra):
        sets = [(pieces, key) for key in keys] + [(swaps, key) for key in swapped]
        arrays = []
        for held, key in sets:
            if not any(held[key][0] is a for a in arrays):
                arrays.append(held[key][0])
        new = lax.optimization_barrier((*arrays, *extra))
        for old, fresh in zip(arrays, new):
            for held in (pieces, swaps):
                for key, (value, unit) in held.items():
                    if value is old:
                        held[key] = (fresh, unit)
        return new[len(arrays) :]

    ways = list(range(len(masks)))
    first, rest = [0, 1], list(range(2, n_col))
    scalars = placement + owned_pattern[0] * CODE
    units = right_units(scalars, owned_rows, n_col, list(range(1, n_col)), 8 * 10**9)
    units = right_units(scalars, owned_rows, n_col, [0], 1) + units

    pieces, swaps = {(0, 0): (units[0], 0)}, {}
    for step in range(1, n_col):
        pieces[step, 0] = (along_col(units[step], step), 0)

    def brought_by(step, way):
        return (step not in first) + way.bit_count() - 1

    def wave(number):
        for at in range(deep):
            keys = [(step, way) for step in rest + first for way in range(1 << at)]
            keys = [key for key in keys if brought_by(*key) == number - 1]
            if keys:
                hop(at, keys)

    def come(number):
        return [(step, way) for step in rest + first for way in ways[1:] if brought_by(step, way) == number]

    def own(keys):
        return [(*pieces[step, way], masks[way], step) for step, way in keys]

    def other(keys):
        return [(*swaps[step, way], crossed(masks[way]), step) for step, way in keys]

    def slots(keys, swapped):
        return [(masks[way], step) for step, way in keys] + [(crossed(masks[way]), step) for step, way in swapped]

    early = [(step, 0) for step in first] + come(0)
    arrived = [(step, 0) for step in rest]
    late = sum([come(number) for number in range(1, deep)], [])
    tail = come(deep)
    ready = early + arrived
    soon = [key for key in late if key[1] <= full // 2 and key[0] in rest]
    then = [key for key in late if key not in soon]
    near = [(0, 0), (1, 0)]
    groups = [(ready, near), ([], [key for key in ready if key not in near]), (late, []), ([], late), (tail, tail)]

    left = left_side(slab_rows, slab_pattern, up(slab_rows.shape[1], 2 * LANES))
    left, point = tied([(1, 0)], [], [left, scalars])
    point = mark(point)
    (point,) = tied([(0, 0), (1, 0)], [], [point])
    wave(0)
    lefts = sides(left, n_col, [slots(*group) for group in groups], point)
    *lefts, point = tied(arrived, [], [*lefts, point])
    point = mark(point)
    (point,) = tied(come(0), [], [point])
    for number in range(1, deep):
        wave(number)
    swap(near)
    swap([key for key in ready if key not in near])
    total = multiply(lefts[0], None, own(ready) + other(near), columns)
    total, point = tied(soon, [], [total, point])
    point = mark(point, 10)
    (point,) = tied(soon, [], [point])
    wave(deep)
    point = mark(point, 5)
    point, total = tied([], [key for key in ready if key not in near], [point, total])
    total = multiply(lefts[1], total, other([key for key in ready if key not in near]), columns, after=[point])
    (total,) = tied(then, [], [total])
    swap(late)
    total = multiply(lefts[2], total, own(late), columns)
    total, point = tied(tail, [], [total, point])
    swap(tail)
    point = mark(point, 8)
    (point,) = tied([], late, [point])
    total = multiply(lefts[3], total, other(late), columns, after=[point])
    return multiply(lefts[4], total, own(tail) + other(tail), columns, final=True)


def solution(mesh):
    return jax.shard_map(
        functools.partial(per_device, mesh.shape["row"], mesh.shape["col"]),
        mesh=mesh,
        in_specs=(
            P("row", None),
            P("row", None),
            P(("row", "col"), None),
            P(("row", "col"), None),
            P(),
        ),
        out_specs=P("row", "col"),
        check_vma=False,
    )
```

```python
import functools

import jax
import jax.numpy as jnp
from jax import lax
from jax.experimental import pallas as pl
from jax.experimental.pallas import tpu as pltpu
from jax.sharding import PartitionSpec as P

BS = 69
LANES = 128
BODY = 64
UNIT = 72
PACK = 16
DEPTH = 256
CODE = 1 << 16
SLOT = 80


def up(n, m):
    return (n + m - 1) // m * m


def moved(load, start, at, width):
    base = start // LANES
    off = start - base * LANES
    first, second = load(base), load(base + 1)
    lane = lax.broadcasted_iota(jnp.int32, first.shape, 1)
    lane_at = at % LANES
    value = pltpu.roll(jnp.where(lane >= off, first, second), lax.rem(lane_at - off + LANES, LANES), 1)
    tile = at // LANES
    pieces = [(tile, value, lane_at, min(lane_at + width, LANES))]
    if lane_at + width > LANES:
        pieces.append((tile + 1, value, 0, lane_at + width - LANES))
    return pieces


def limit(need):
    return pltpu.CompilerParams(vmem_limit_bytes=min(need + 8 * 2**20, 60 * 2**20))


def crossed(mask):
    return (1 ^ mask[1], 1 ^ mask[0])


def unit_size(columns):
    full, over = columns // LANES, columns % LANES
    return full * BODY // PACK + pl.cdiv(full, PACK // (BS - BODY)) + pl.cdiv(pl.cdiv(3 * over, LANES) * (UNIT // 3), PACK)


def pack_unit(out, tiles, columns):
    full, over = columns // LANES, columns % LANES
    at = 0
    for tile in tiles[:full]:
        for row in range(0, BODY, PACK):
            out[at] = tile[row : row + PACK].astype(jnp.bfloat16)
            at += 1
    few = BS - BODY
    for t in range(0, full, PACK // few):
        rows = jnp.zeros((PACK, LANES), jnp.float32)
        for k, tile in enumerate(tiles[t : min(full, t + PACK // few)]):
            rows += pltpu.roll(jnp.concatenate([tile[BODY:], jnp.zeros((PACK + BODY - UNIT, LANES), jnp.float32)], 0), k * few, 0)
        out[at] = rows.astype(jnp.bfloat16)
        at += 1
    if not over:
        return
    third = UNIT // 3
    lane = lax.broadcasted_iota(jnp.int32, (third, LANES), 1)
    packed = [jnp.zeros((third, LANES), jnp.float32) for _ in range(pl.cdiv(3 * over, LANES))]
    for g in range(3):
        value = tiles[full][g * third : (g + 1) * third]
        t, shift = g * over // LANES, g * over % LANES
        if shift:
            value = pltpu.roll(value, shift, 1)
        packed[t] = jnp.where((lane >= shift) & (lane < shift + over), value, packed[t])
        if shift + over > LANES:
            packed[t + 1] = jnp.where(lane < shift + over - LANES, value, packed[t + 1])
    rows = jnp.concatenate(packed, 0)
    if rows.shape[0] % PACK:
        rows = jnp.concatenate([rows, jnp.zeros((PACK - rows.shape[0] % PACK, LANES), jnp.float32)], 0)
    for row in range(0, rows.shape[0], PACK):
        out[at] = rows[row : row + PACK].astype(jnp.bfloat16)
        at += 1


def unpack_unit(right, first, piece, at, columns):
    full, over = columns // LANES, columns % LANES
    for t in range(full):
        for row in range(0, BODY, PACK):
            right[first + row : first + row + PACK, t * LANES : (t + 1) * LANES] = piece[at]
            at += 1
    few = BS - BODY
    row = lax.broadcasted_iota(jnp.int32, (PACK, LANES), 0)
    for t in range(0, full, PACK // few):
        rows = piece[at].astype(jnp.float32)
        at += 1
        for k in range(min(PACK // few, full - t)):
            mine = pltpu.roll(rows, PACK - k * few, 0) if k else rows
            mine = jnp.where(row < few, mine, 0.0).astype(jnp.bfloat16)
            right[first + BODY : first + BODY + PACK, (t + k) * LANES : (t + k + 1) * LANES] = mine
    if not over:
        return
    third = UNIT // 3
    count = pl.cdiv(3 * over, LANES)
    rows = jnp.concatenate([piece[at + i].astype(jnp.float32) for i in range(pl.cdiv(count * third, PACK))], 0)
    packed = [rows[i * third : (i + 1) * third] for i in range(count)]
    lane = lax.broadcasted_iota(jnp.int32, (third, LANES), 1)
    values = []
    for g in range(3):
        t, shift = g * over // LANES, g * over % LANES
        value = packed[t]
        if shift:
            value = pltpu.roll(value, LANES - shift, 1)
        if shift + over > LANES:
            value = jnp.where(lane < LANES - shift, value, pltpu.roll(packed[t + 1], LANES - shift, 1))
        values.append(value)
    values.append(jnp.zeros((SLOT - UNIT, LANES), jnp.float32))
    right[first : first + SLOT, full * LANES : (full + 1) * LANES] = jnp.concatenate(values, 0).astype(jnp.bfloat16)


def right_kernel(n_col, steps, scalars, raw, *refs):
    outs, rows = refs[-1 - len(steps) : -1], refs[-1]
    rows[: raw.shape[0], : raw.shape[1]] = raw[...]
    columns = raw.shape[1] // n_col
    here = scalars.shape[0] // n_col
    me = lax.axis_index("col")
    shape = (UNIT, LANES)
    lane = lax.broadcasted_iota(jnp.int32, shape, 1)
    real = lax.broadcasted_iota(jnp.int32, shape, 0) < BS

    def load(tile):
        return rows[:, pl.ds(pl.multiple_of(tile * LANES, LANES), LANES)].astype(jnp.float32)

    for out, step in zip(outs, steps):
        tiles = [jnp.zeros(shape, jnp.float32) for _ in range(pl.cdiv(columns, LANES))]
        for t in range(here):
            source = scalars[(me ^ step) * here + t] & (CODE - 1)
            keep = real & (jnp.full(shape, scalars[source]) >= CODE)
            for tile, value, lo, hi in moved(load, source * BS, t * BS, BS):
                tiles[tile] = jnp.where((lane >= lo) & (lane < hi) & keep, value, tiles[tile])
        pack_unit(out, tiles, columns)


def right_units(scalars, owned_rows, n_col, steps, weight):
    columns = owned_rows.shape[1]
    size = unit_size(columns // n_col)
    return pl.pallas_call(
        functools.partial(right_kernel, n_col, steps),
        out_shape=[jax.ShapeDtypeStruct((size, PACK, LANES), jnp.bfloat16)] * len(steps),
        in_specs=[pl.BlockSpec(memory_space=pltpu.SMEM)] + [pl.BlockSpec(memory_space=pltpu.VMEM)],
        out_specs=[pl.BlockSpec(memory_space=pltpu.VMEM)] * len(steps),
        scratch_shapes=[pltpu.VMEM((UNIT, up(columns, LANES) + LANES), jnp.bfloat16)],
        compiler_params=limit(2**22),
        cost_estimate=pl.CostEstimate(flops=weight, bytes_accessed=1, transcendentals=0),
        name="right_units",
    )(scalars, owned_rows)


def left_kernel(high, pattern, rows_in, out, rows, sems):
    height, columns = rows_in.shape
    block_rows, depth = pattern.shape
    width = out.shape[1]
    count = height // high

    def copy(i):
        return pltpu.make_async_copy(rows_in.at[pl.ds(i * high, high), :], rows.at[pl.ds(i * high, high), :], sems.at[i])

    for i in range(count):
        copy(i).start()
    lane = lax.broadcasted_iota(jnp.int32, (depth, width), 1)
    block = lax.broadcasted_iota(jnp.int32, (depth, width), 0) * BS
    spread = jnp.where((lane >= block) & (lane < block + BS), 1.0, 0.0).astype(jnp.bfloat16)
    by_block = jnp.dot(pattern[...].astype(jnp.bfloat16), spread, preferred_element_type=jnp.float32)
    for at in range(0, width, LANES):
        wide = min(LANES, columns - at)
        if wide <= 0:
            out[:, at:] = jnp.zeros((height, width - at), jnp.bfloat16)
            break
        if wide < LANES:
            out[:, at : at + LANES] = jnp.zeros((height, LANES), jnp.bfloat16)
    row = lax.broadcasted_iota(jnp.int32, (PACK, columns), 0)
    keeps = {}

    def keep(b):
        if b not in keeps:
            keeps.clear()
            keeps[b] = jnp.broadcast_to(by_block[b : b + 1, :columns], (PACK, columns)).astype(jnp.bfloat16)
        return keeps[b]

    for first in range(0, height, PACK):
        if first % high == 0:
            copy(first // high).wait()
        own, edge = first // BS, (first // BS + 1) * BS
        mask = keep(own)
        if edge < first + PACK:
            mask = jnp.where(row < edge - first, mask, keep(own + 1))
        out[first : first + PACK, :columns] = rows[first : first + PACK, :] * mask


def left_side(slab_rows, slab_pattern, width):
    height, columns = slab_rows.shape
    high = 368
    return pl.pallas_call(
        functools.partial(left_kernel, high),
        out_shape=jax.ShapeDtypeStruct((height, width), jnp.bfloat16),
        in_specs=[pl.BlockSpec(memory_space=pltpu.VMEM), pl.BlockSpec(memory_space=pltpu.HBM)],
        out_specs=pl.BlockSpec(memory_space=pltpu.VMEM),
        scratch_shapes=[pltpu.VMEM((height, columns), jnp.bfloat16), pltpu.SemaphoreType.DMA((height // high,))],
        compiler_params=limit(height * (width + columns) * 2),
        cost_estimate=pl.CostEstimate(flops=1, bytes_accessed=1, transcendentals=0),
        name="left_side",
    )(slab_pattern, slab_rows)


def place(slot):
    return slot // 3 * DEPTH + slot % 3 * SLOT


def side_kernel(n_col, groups, left, point, *refs):
    outs, pick = refs[: len(groups)], refs[-1]
    high = 368
    col = lax.broadcasted_iota(jnp.int32, (DEPTH, DEPTH), 1)
    ahead = lax.broadcasted_iota(jnp.int32, (DEPTH, DEPTH), 0) - col
    turn = 0
    for out, slots in zip(outs, groups):
        for first in range(0, len(slots), 3):
            tiles = []
            base = turn % 2 * 3 * DEPTH
            turn += 1
            for t, (mask, step) in enumerate(slots[first : first + 3]):
                start = block_of(n_col, mask, step) * BS
                tile = start // LANES
                tiles.append(pl.multiple_of(tile * LANES, LANES))
                at = t * SLOT
                hit = (ahead == start - tile * LANES - at) & (col >= at) & (col < at + BS)
                pick[base + t * DEPTH : base + (t + 1) * DEPTH, :] = jnp.where(hit, 1.0, 0.0).astype(jnp.bfloat16)
            for at in range(0, left.shape[0], high):
                total = None
                for t, tile in enumerate(tiles):
                    some = pick[base + t * DEPTH : base + (t + 1) * DEPTH, :]
                    part = jnp.dot(left[at : at + high, pl.ds(tile, DEPTH)], some, preferred_element_type=jnp.float32)
                    total = part if total is None else total + part
                out[at : at + high, first // 3 * DEPTH : (first // 3 + 1) * DEPTH] = total.astype(jnp.bfloat16)


def sides(left, n_col, groups, point):
    height = left.shape[0]
    widths = [up(len(slots), 3) // 3 * DEPTH for slots in groups]
    return pl.pallas_call(
        functools.partial(side_kernel, n_col, groups),
        out_shape=[jax.ShapeDtypeStruct((height, width), jnp.bfloat16) for width in widths],
        in_specs=[pl.BlockSpec(memory_space=pltpu.VMEM), pl.BlockSpec(memory_space=pl.ANY)],
        out_specs=[pl.BlockSpec(memory_space=pltpu.VMEM)] * len(groups),
        scratch_shapes=[pltpu.VMEM((6 * DEPTH, DEPTH), jnp.bfloat16)],
        compiler_params=limit(height * (sum(widths) + left.shape[1]) * 2),
        cost_estimate=pl.CostEstimate(flops=1, bytes_accessed=1, transcendentals=0),
        name="sides",
    )(left, point)


def block_of(n_col, mask, step):
    me = lax.axis_index("row")
    return (me ^ jnp.where(me & 1 == 0, mask[0], mask[1])) * n_col + (lax.axis_index("col") ^ step)


def listed(units):
    pieces, places = [], []
    for piece, *_ in units:
        at = next((i for i, p in enumerate(pieces) if p is piece), None)
        if at is None:
            at = len(pieces)
            pieces.append(piece)
        places.append(at)
    return pieces, places


def row_tiles(height, final):
    starts = list(range(0, height, 368))
    if final and height - starts[-1] == 368:
        starts.append(height - 128)
    return [(at, end - at) for at, end in zip(starts, starts[1:] + [height])]


def multiply_kernel(places, columns, with_total, final, left, *refs):
    out, right = refs[len(refs) - 4 :][:2] if final else refs[-2:]
    pieces = refs[with_total:]
    for first in range(0, right.shape[0], DEPTH):
        used = min(3, len(places) - first // DEPTH * 3) * SLOT
        right[first + used : first + DEPTH, :] = jnp.zeros((DEPTH - used, right.shape[1]), right.dtype)
    for slot, (piece, unit) in enumerate(places):
        unpack_unit(right, place(slot), pieces[piece], unit * unit_size(columns), columns)
    copies = []
    for at, high in row_tiles(left.shape[0], final):
        value = jnp.dot(left[at : at + high, :], right[...], preferred_element_type=jnp.float32)
        if with_total:
            value += refs[0][at : at + high, :]
        if final:
            tiles, sems = refs[-2:]
            tiles[at : at + high, :] = value[:, : tiles.shape[1]].astype(tiles.dtype)
            copies.append(pltpu.make_async_copy(tiles.at[pl.ds(at, high)], out.at[pl.ds(at, high)], sems.at[len(copies)]))
            copies[-1].start()
        else:
            out[at : at + high, :] = value
    for copy in copies:
        copy.wait()


def multiply(left, total, units, columns, final=False, after=()):
    height, width = left.shape
    pieces, places = listed(units)
    wide = up(columns, LANES)
    operands = [left] + ([] if total is None else [total]) + pieces
    memory = [pltpu.VMEM] * len(operands) + [pl.ANY] * len(after)
    scratch = [pltpu.VMEM((width, wide), jnp.bfloat16)]
    if final:
        scratch += [pltpu.VMEM((height, columns), jnp.bfloat16), pltpu.SemaphoreType.DMA((len(row_tiles(height, True)),))]
    return pl.pallas_call(
        functools.partial(multiply_kernel, [(at, unit[1]) for at, unit in zip(places, units)], columns, total is not None, final),
        out_shape=jax.ShapeDtypeStruct((height, columns if final else wide), jnp.bfloat16 if final else jnp.float32),
        in_specs=[pl.BlockSpec(memory_space=space) for space in memory],
        out_specs=pl.BlockSpec(memory_space=pltpu.HBM if final else pltpu.VMEM),
        scratch_shapes=scratch,
        compiler_params=limit(width * wide * 2 + height * (wide * 6 + width * 2) + sum(p.size for p in pieces) * 2),
        cost_estimate=pl.CostEstimate(flops=1, bytes_accessed=1, transcendentals=0),
        name="multiply",
    )(*operands, *after)


def mark_kernel(value, out):
    pass


def mark(value, weight=3):
    return pl.pallas_call(
        mark_kernel,
        out_shape=jax.ShapeDtypeStruct(value.shape, value.dtype),
        in_specs=[pl.BlockSpec(memory_space=pl.ANY)],
        out_specs=pl.BlockSpec(memory_space=pl.ANY),
        input_output_aliases={0: 0},
        compiler_params=pltpu.CompilerParams(vmem_limit_bytes=2**20),
        cost_estimate=pl.CostEstimate(flops=weight * 10**9, bytes_accessed=1, transcendentals=0),
        name="mark",
    )(value)


def per_device(n_row, n_col, slab_rows, slab_pattern, owned_rows, owned_pattern, placement):
    columns = owned_rows.shape[1] // n_col
    size = unit_size(columns)
    bits = [1 << b for b in range(1, n_row.bit_length() - 1)]
    moves = list(zip(bits, bits[::-1]))
    last, deep = n_col - 1, len(moves)

    def along_row(value, move):
        return lax.ppermute(value, "row", [(i, i ^ move[i & 1]) for i in range(n_row)])

    def along_col(value, step):
        return lax.ppermute(value, "col", [(i, i ^ step) for i in range(n_col)])

    masks = [(0, 0)]
    for move in moves:
        masks += [(m[0] ^ move[0], m[1] ^ move[1]) for m in masks]

    full = len(masks) - 1

    def unit_of(key):
        value, unit = pieces[key]
        return value if value.shape[0] == size else value[unit * size : (unit + 1) * size]

    def joined(keys):
        value = pieces[keys[0]][0]
        if value.shape[0] == size * len(keys) and all(pieces[k][0] is value and pieces[k][1] == i for i, k in enumerate(keys)):
            return value
        return jnp.concatenate([unit_of(key) for key in keys]) if len(keys) > 1 else unit_of(keys[0])

    def hop(at, keys):
        sent = along_row(joined(keys), moves[at])
        for unit, (step, way) in enumerate(keys):
            pieces[step, way | 1 << at] = (sent, unit)

    def swap(keys):
        other = along_row(joined(keys), (1, 1))
        for unit, key in enumerate(keys):
            swaps[key] = (other, unit)

    def tied(keys, swapped, extra):
        sets = [(pieces, key) for key in keys] + [(swaps, key) for key in swapped]
        arrays = []
        for held, key in sets:
            if not any(held[key][0] is a for a in arrays):
                arrays.append(held[key][0])
        new = lax.optimization_barrier((*arrays, *extra))
        for old, fresh in zip(arrays, new):
            for held in (pieces, swaps):
                for key, (value, unit) in held.items():
                    if value is old:
                        held[key] = (fresh, unit)
        return new[len(arrays) :]

    ways = list(range(len(masks)))
    first, rest = [0, 1], list(range(2, n_col))
    scalars = placement + owned_pattern[0] * CODE
    units = right_units(scalars, owned_rows, n_col, list(range(1, n_col)), 8 * 10**9)
    units = right_units(scalars, owned_rows, n_col, [0], 1) + units

    pieces, swaps = {(0, 0): (units[0], 0)}, {}
    for step in range(1, n_col):
        pieces[step, 0] = (along_col(units[step], step), 0)

    def brought_by(step, way):
        return (step not in first) + way.bit_count() - 1

    def wave(number):
        for at in range(deep):
            keys = [(step, way) for step in rest + first for way in range(1 << at)]
            keys = [key for key in keys if brought_by(*key) == number - 1]
            if keys:
                hop(at, keys)

    def come(number):
        return [(step, way) for step in rest + first for way in ways[1:] if brought_by(step, way) == number]

    def own(keys):
        return [(*pieces[step, way], masks[way], step) for step, way in keys]

    def other(keys):
        return [(*swaps[step, way], crossed(masks[way]), step) for step, way in keys]

    def slots(keys, swapped):
        return [(masks[way], step) for step, way in keys] + [(crossed(masks[way]), step) for step, way in swapped]

    early = [(step, 0) for step in first] + come(0)
    arrived = [(step, 0) for step in rest]
    late = sum([come(number) for number in range(1, deep)], [])
    tail = come(deep)
    ready = early + arrived
    soon = [key for key in late if key[1] <= full // 2 and key[0] in rest]
    then = [key for key in late if key not in soon]
    near = [(0, 0), (1, 0)]
    far = [key for key in ready if key not in near]
    groups = [(ready, near), (soon, far), (then, soon), (tail, then), ([], tail)]

    left = left_side(slab_rows, slab_pattern, up(slab_rows.shape[1], 2 * LANES))
    left, point = tied([(1, 0)], [], [left, scalars])
    point = mark(point)
    (point,) = tied([(0, 0), (1, 0)], [], [point])
    wave(0)
    lefts = sides(left, n_col, [slots(*group) for group in groups], point)
    *lefts, point = tied(arrived, [], [*lefts, point])
    point = mark(point)
    (point,) = tied(come(0), [], [point])
    for number in range(1, deep):
        wave(number)
    swap(near)
    swap([key for key in ready if key not in near])
    total = multiply(lefts[0], None, own(ready) + other(near), columns)
    total, point = tied(soon, [], [total, point])
    point = mark(point, 10)
    (point,) = tied(soon, [], [point])
    wave(deep)
    point = mark(point, 5)
    point, total = tied([], [key for key in ready if key not in near], [point, total])
    total = multiply(lefts[1], total, own(soon) + other(far), columns, after=[point])
    (total,) = tied(then, [], [total])
    swap(soon)
    swap(then)
    total = multiply(lefts[2], total, own(then) + other(soon), columns)
    total, point = tied(tail, [], [total, point])
    swap(tail)
    point = mark(point, 5)
    (point,) = tied([], then, [point])
    total = multiply(lefts[3], total, own(tail) + other(then), columns, after=[point])
    return multiply(lefts[4], total, other(tail), columns, final=True)


def solution(mesh):
    return jax.shard_map(
        functools.partial(per_device, mesh.shape["row"], mesh.shape["col"]),
        mesh=mesh,
        in_specs=(
            P("row", None),
            P("row", None),
            P(("row", "col"), None),
            P(("row", "col"), None),
            P(),
        ),
        out_specs=P("row", "col"),
        check_vma=False,
    )
```
